32 devices in a mesh: groups: 2 (over y), ep: 8 (over z, x), tp: 2 (over core).
Axes of the slice: x: 2, y: 2, z: 4, core: 2. Of those that a mesh axis runs over, the one named last changes fastest.
Arguments:
- residual: bfloat16 [512, 7168], P(('groups', 'ep'), 'tp'), parts along dimension 0
- attn_partial: bfloat16 [2, 512, 7168], P('tp', ('groups', 'ep')), parts along dimension 1, may hold values from -6 to 6
- norm_gain: float32 [7168], P('tp'), may hold values from 0.1 to 1.9
- route_ids: int32 [512, 8], P(('groups', 'ep')), parts along dimension 0, may hold values from 0 to 255, as said below
- route_scores: float32 [512, 8], P(('groups', 'ep')), parts along dimension 0, may hold values from 0.05 to 1
- w_in: bfloat16 [8, 7168, 4096], P('ep', 'tp'), may hold values from -0.0625 to 0.0625
- w_down: bfloat16 [8, 2048, 7168], P('ep', None, 'tp'), may hold values from -0.125 to 0.125
Outputs:
- stream: bfloat16 [512, 7168], P(('groups', 'ep'), 'tp'), parts along dimension 0
- moe_out: bfloat16 [512, 7168], P(('groups', 'ep'), 'tp'), parts along dimension 0
The draws below stay inside these ranges and needn't reach their ends.
There are 2 independent parts, one for each index of `groups`. The reference program is written for one: setup_inputs(seed, part) draws one part's arguments, and reference() takes and returns one part's arrays. A program takes and returns all parts, laid end to end along the dimension named above; an argument that names none is the same for every part. Nothing has to cross between parts.
Inputs may be any that keep to these rules, and one draw needn't show every extreme that they name: `route_ids`: each row names 8 different experts. In each aligned block of 32 rows (the rows of one device) one expert below 8, the same in all blocks, is named by exactly 2 rows, and every other expert below 8 by exactly one row.
All inputs are finite; a program needn't handle non-finite values.
Results may differ from the reference program's by a relative error of at most 0.0076.
Values may be sent and summed in bfloat16 or wider, within the bound.
A program may use at most 320 MiB of HBM per device.

```python
import math
import jax
import jax.numpy as jnp
from jax import lax

D = 7168
FF = 2048
ROUTED = 256
TOP = 8
EXP = 8
TOK_DEV = 32
TOKENS = 256
SLICES = 1
H_DEV = 2048
CAP = 2
SLOTS = 16
N_TP = 2


def draw_residual(key, part):
    key = jax.random.fold_in(key, 5)
    key_list = jax.random.split(key, 3)
    base_values = jax.random.normal(key_list[0], (TOKENS, D), jnp.float32)
    lower_end = 0.3
    upper_end = 3.0
    row_scale = jnp.exp(jax.random.uniform(key_list[1], (TOKENS, 1), jnp.float32, math.log(lower_end), math.log(upper_end)))
    column_scale = jnp.exp(jax.random.uniform(key_list[2], (1, D), jnp.float32, math.log(lower_end), math.log(upper_end)))
    return (base_values * row_scale * column_scale).astype(jnp.bfloat16)


def draw_route_ids(key, part):
    key = jax.random.fold_in(key, 11)
    key_list = jax.random.split(key, 5)
    blocks = TOKENS // TOK_DEV
    hottest = jax.random.randint(key_list[0], (), 0, EXP)
    counts = jnp.ones((blocks, EXP), jnp.int32)
    counts = jnp.where(jnp.arange(EXP)[None, :] == hottest, CAP, counts)
    tiebreak = jax.random.randint(key_list[2], (blocks, EXP, TOK_DEV), 0, 2 ** 16) * TOK_DEV + jnp.arange(TOK_DEV)
    ranking = jnp.argsort(jnp.argsort(tiebreak, axis=2), axis=2)
    chosen = jnp.transpose(ranking < counts[:, :, None], (0, 2, 1)).reshape(TOKENS, EXP)
    expert_ids = jnp.arange(ROUTED, dtype=jnp.int32)
    noise_keys = jax.random.randint(key_list[3], (TOKENS, ROUTED), 0, 2 ** 14) * ROUTED + expert_ids
    window = jnp.where(chosen, noise_keys[:, :EXP] + 2 ** 23, -1 - expert_ids[:EXP])
    ranked = jnp.concatenate([window, noise_keys[:, EXP:]], axis=1).astype(jnp.int32)
    top_values, picked = lax.top_k(ranked, TOP)
    shuffle = jax.random.randint(key_list[4], (TOKENS, TOP), 0, 2 ** 14) * TOP + jnp.arange(TOP)
    return jnp.take_along_axis(picked, jnp.argsort(shuffle, axis=1), axis=1).astype(jnp.int32)


def shard_levels(stream_key, shape, cuts, low, high):
    def one(dim, parts):
        draws = jax.random.uniform(jax.random.fold_in(jax.random.fold_in(stream_key, 6), dim), (parts,), jnp.float32, low / len(cuts), high / len(cuts))
        return jnp.repeat(jnp.exp(draws), shape[dim] // parts).reshape((-1,) + (1,) * (len(shape) - dim - 1))

    loudness = one(*cuts[0])
    for cut in cuts[1:]:
        loudness = loudness * one(*cut)
    return loudness


def bell_draw(key, extent, scale, most, cuts=(), kind=jnp.bfloat16):
    entries = jax.random.normal(key, extent, jnp.float32) * scale
    if len(cuts) > 0:
        entries = shard_levels(key, extent, cuts, -0.22, 0.18) * entries
    return jnp.clip(entries, min=-most, max=most).astype(kind)


def setup_inputs(seed: int = 0, part: int = 0) -> dict:
    key_of = jax.random.split(jax.random.key(seed), 8)
    part_keys = jax.random.split(jax.random.fold_in(key_of[7], part), 8)
    residual = draw_residual(jax.random.fold_in(jax.random.fold_in(key_of[7], part), 71), part)
    attn_partial = bell_draw(part_keys[1], (N_TP, TOKENS, D), 1.0, 6.0, ((0, 2), (1, 8)))
    norm_gain = jnp.clip(1.0 + 0.18 * jax.random.normal(key_of[2], (D,), jnp.float32), 0.1, 1.9)
    route_ids = draw_route_ids(jax.random.fold_in(jax.random.fold_in(key_of[7], part), 71), part)
    route_scores = jnp.clip(0.05 + 0.95 * jax.random.uniform(part_keys[4], (TOKENS, TOP), jnp.float32) ** shard_levels(part_keys[4], (TOKENS, TOP), ((0, 8),), -0.2, 0.2), 0.05, 1.0)
    w_in = bell_draw(key_of[5], (EXP * SLICES, D, 2 * H_DEV), D ** -0.5, 0.0625, ((0, 8), (1, 2)))
    w_down = bell_draw(key_of[6], (EXP * SLICES, H_DEV, D), FF ** -0.5, 0.125, ((0, 8), (2, 2)))
    return dict(residual=residual, attn_partial=attn_partial, norm_gain=norm_gain, route_ids=route_ids, route_scores=route_scores, w_in=w_in, w_down=w_down)


route_scale = 2.5
norm_eps = 1e-06

def reference(residual, attn_partial, norm_gain, route_ids, route_scores, w_in, w_down):
    summed = residual.astype(jnp.float32) + lax.optimization_barrier(jnp.sum(attn_partial.astype(jnp.float32), axis=0))
    stream = lax.optimization_barrier(summed.astype(jnp.bfloat16))
    wide_rows = stream.astype(jnp.float32)
    mean_square = lax.optimization_barrier(jnp.mean(wide_rows * wide_rows, axis=1, keepdims=True))
    normed = (wide_rows * lax.rsqrt(mean_square + norm_eps) * norm_gain).astype(jnp.bfloat16)
    scores = route_scores.astype(jnp.float32)
    shares = route_scale * scores / lax.optimization_barrier(jnp.sum(scores, axis=1, keepdims=True))
    token_index = jnp.arange(TOKENS, dtype=jnp.int32)
    slot_index = jnp.arange(SLOTS, dtype=jnp.int32)

    def add_expert(expert_index, running):
        picked = route_ids == expert_index
        weight_row = lax.optimization_barrier(jnp.sum(jnp.where(picked, shares, 0.0), axis=1))
        member = jnp.any(picked, axis=1)
        flags = member.astype(jnp.int32)
        position = (jnp.cumsum(flags) - 1).astype(jnp.int32)
        target = jnp.where(member, position, SLOTS).astype(jnp.int32)
        gather_order = jnp.zeros((SLOTS,), jnp.int32).at[target].set(token_index, mode='drop')
        valid_rows = slot_index < jnp.sum(flags).astype(jnp.int32)
        block_rows = normed[gather_order]
        start = (expert_index * SLICES).astype(jnp.int32)
        block_in = lax.dynamic_slice_in_dim(w_in, start, SLICES, 0)
        gate_matrix = jnp.transpose(block_in[:, :, :H_DEV], (1, 0, 2)).reshape(D, FF)
        up_matrix = jnp.transpose(block_in[:, :, H_DEV:], (1, 0, 2)).reshape(D, FF)
        down_matrix = lax.dynamic_slice_in_dim(w_down, start, SLICES, 0).reshape(FF, D)
        gate_values = jnp.dot(block_rows, gate_matrix, preferred_element_type=jnp.float32)
        up_values = jnp.dot(block_rows, up_matrix, preferred_element_type=jnp.float32)
        active = (jax.nn.silu(gate_values) * up_values).astype(jnp.bfloat16)
        result = jnp.dot(active, down_matrix, preferred_element_type=jnp.float32)
        scaled = jnp.where(valid_rows[:, None], result * weight_row[gather_order][:, None], 0.0)
        return running.at[gather_order].add(scaled)
    total = lax.fori_loop(0, EXP, add_expert, jnp.zeros((TOKENS, D), jnp.float32))
    return (stream, total.astype(jnp.bfloat16))
```

```python
import functools

import jax
import jax.numpy as jnp
from jax import lax
from jax.experimental import pallas as pl
from jax.experimental.pallas import tpu as pltpu
from jax.sharding import PartitionSpec as P

EXP = 8
CAP = 2
CH = 512
MESH = pl.DeviceIdType.MESH

route_scale = 2.5
norm_eps = 1e-06


def iota(shape, dim):
    return lax.broadcasted_iota(jnp.int32, shape, dim)


def each(count, body):
    if count <= 8:
        for step in range(count):
            body(step)
    else:

        def run(step, carry):
            body(step)
            return carry

        lax.fori_loop(0, count, run, 0)


def split_two(value):
    high = value.astype(jnp.bfloat16)
    return high, (value - high.astype(jnp.float32)).astype(jnp.bfloat16)


def route_tables(ids, scores, rows):
    wide = 8 * rows
    spread = (iota((rows, wide), 0) == (iota((rows, wide), 1) & (rows - 1))).astype(jnp.float32)
    turn = (((0,), (0,)), ((), ()))
    ids_t = lax.dot_general(
        ids.astype(jnp.float32).astype(jnp.bfloat16),
        spread.astype(jnp.bfloat16),
        turn,
        preferred_element_type=jnp.float32,
    )
    scores_t = lax.dot_general(
        scores,
        spread,
        turn,
        precision=lax.Precision.HIGHEST,
        preferred_element_type=jnp.float32,
    )
    shares = route_scale * scores_t / jnp.sum(scores_t, axis=0, keepdims=True)
    expert = iota((EXP, wide), 0).astype(jnp.float32)
    member = jnp.zeros((EXP, wide), jnp.float32)
    weight = jnp.zeros((EXP, wide), jnp.float32)
    for k in range(ids.shape[1]):
        hit = ids_t[k : k + 1, :] == expert
        member = jnp.where(hit, 1.0, member)
        weight = weight + jnp.where(hit, shares[k : k + 1, :], 0.0)
    earlier = iota((wide, wide), 0) < (iota((wide, wide), 1) & (rows - 1))
    rank = jnp.dot(
        member.astype(jnp.bfloat16),
        earlier.astype(jnp.float32).astype(jnp.bfloat16),
        preferred_element_type=jnp.float32,
    )
    code = jnp.where(member > 0.0, rank, -1.0)
    line = iota((16, wide), 0)
    same_chunk = (line >> 1) == (iota((16, wide), 1) // rows)
    want = jnp.where(same_chunk, (line & 1).astype(jnp.float32), -2.0)
    places, weighted = [], []
    for e in range(EXP):
        on = jnp.where(code[e : e + 1, :] == want, 1.0, 0.0)
        places.append(on)
        weighted.append(on * weight[e : e + 1, :])
    return jnp.concatenate(places, axis=0), jnp.concatenate(weighted, axis=0)


def kernel(
    ep,
    res_hbm, attn_hbm, gain_hbm, ids_hbm, scores_hbm, w_in_hbm, w_down_hbm,
    stream_hbm, moe_hbm,
    w_in, w_down, res, attn_own, attn_peer, gain, ids, scores,
    stream, moe, stacked, packed, recv, tokens, h_own, h_peer, sq_own, sq_peer,
    act, y_stack, y_packed, ret, weights_hi, weights_lo,
    in_sem, w_in_sem, w_down_sem, out_sem, tp_send, tp_recv,
    h_send, h_recv, go_send, go_recv, back_send, back_recv,
):
    rows, half = res.shape
    chunks = half // CH
    pieces = ep // EXP
    hidden = w_in.shape[1] // 2
    blocks, slots, _ = h_own.shape
    hb = hidden // blocks
    me = lax.axis_index("ep")
    core = lax.axis_index("tp")
    peer = 1 - core

    def local(src, dst, sem):
        copy = pltpu.make_async_copy(src, dst, sem)
        copy.start()
        return copy

    own_cols = pl.ds(pl.multiple_of(core * half, 128), half)
    peer_cols = pl.ds(pl.multiple_of(peer * half, 128), half)
    barrier = pltpu.get_barrier_semaphore()
    pl.semaphore_signal(barrier, inc=1, device_id={"tp": peer}, device_id_type=MESH)

    def greet(step):
        other = lax.rem(me + step + 1, ep)
        pl.semaphore_signal(barrier, inc=1, device_id={"ep": other}, device_id_type=MESH)

    each(ep - 1, greet)
    copy_ids = local(ids_hbm, ids, in_sem.at[0])
    copy_scores = local(scores_hbm, scores, in_sem.at[1])
    copy_attn = local(attn_hbm.at[0, :, own_cols], attn_own, in_sem.at[2])
    copy_res = local(res_hbm, res, in_sem.at[3])
    copy_gain = local(gain_hbm, gain, in_sem.at[4])
    copies_in, copies_down = [], []
    for b in range(blocks):
        for part in range(2):
            cols = pl.ds(part * hidden + b * hb, hb)
            copies_in.append(
                local(w_in_hbm.at[0, :, cols], w_in.at[:, cols], w_in_sem.at[2 * b + part])
            )
    for c in range(chunks):
        cols = pl.ds(c * CH, CH)
        copies_down.append(local(w_down_hbm.at[0, :, cols], w_down.at[:, cols], w_down_sem.at[c]))

    pl.semaphore_wait(barrier, ep)
    swap = pltpu.make_async_remote_copy(
        src_ref=attn_hbm.at[0, :, peer_cols],
        dst_ref=attn_peer,
        send_sem=tp_send.at[0],
        recv_sem=tp_recv.at[0],
        device_id={"tp": peer},
        device_id_type=MESH,
    )
    swap.start()

    copy_ids.wait()
    copy_scores.wait()
    place, weighted = route_tables(ids[...], scores[...], rows)
    weights_hi[...], weights_lo[...] = split_two(weighted.T)
    place = place.astype(jnp.bfloat16)
    side = iota((128, 128), 0)
    swapped = ((side & 14) << 3) | ((side >> 4) << 1) | (side & 1)
    shuffle = (swapped == iota((128, 128), 1)).astype(jnp.float32).astype(jnp.bfloat16)

    copy_attn.wait()
    copy_res.wait()
    copy_gain.wait()
    swap.wait()

    total = res[...].astype(jnp.float32) + (
        attn_own[...].astype(jnp.float32) + attn_peer[...].astype(jnp.float32)
    )
    stream[...] = total.astype(jnp.bfloat16)
    out_stream = local(stream, stream_hbm, out_sem.at[0])
    wide = stream[...].astype(jnp.float32)
    square = jnp.sum(wide * wide, axis=1, keepdims=True)
    scaled = wide * lax.rsqrt(square * (1.0 / half) + norm_eps) * gain[...]
    scaled = scaled.astype(jnp.bfloat16)
    for c in range(chunks):
        stacked[c * rows : (c + 1) * rows, :] = scaled[:, c * CH : (c + 1) * CH]
    square = jnp.minimum(square, 3.0e38)
    first = square.astype(jnp.bfloat16).astype(jnp.float32)
    second = (square - first).astype(jnp.bfloat16).astype(jnp.float32)
    third = square - first - second
    lane = iota((rows, CH), 1)
    terms = jnp.where(
        lane == 0, first, jnp.where(lane == 1, second, jnp.where(lane == 2, third, 0.0))
    )
    stacked[chunks * rows :, :] = terms.astype(jnp.bfloat16)
    sent = jnp.dot(place, stacked[...], preferred_element_type=jnp.float32)
    packed[...] = sent.astype(jnp.bfloat16).reshape(packed.shape)

    def go(step):
        other = lax.rem(me + step + 1, ep)
        return pltpu.make_async_remote_copy(
            src_ref=packed.at[other // pieces],
            dst_ref=recv.at[me],
            send_sem=go_send.at[other],
            recv_sem=go_recv.at[me],
            device_id={"ep": other},
            device_id_type=MESH,
        )

    def arrive(step):
        other = lax.rem(me + step + 1, ep)
        pltpu.make_async_remote_copy(
            src_ref=packed.at[0],
            dst_ref=recv.at[other],
            send_sem=go_send.at[other],
            recv_sem=go_recv.at[other],
            device_id={"ep": other},
            device_id_type=MESH,
        ).wait_recv()

    each(ep - 1, lambda step: go(step).start())
    recv[me] = packed[me // pieces]
    y_stack[:, chunks * 16 :, :] = jnp.zeros((ep // 8, 16, CH), jnp.bfloat16)
    each(ep - 1, arrive)

    for k in range(ep // 8):
        block = recv[8 * k : 8 * k + 8].reshape(128, CH)
        order = jnp.dot(shuffle, block, preferred_element_type=jnp.float32)
        for c in range(chunks):
            tokens[16 * k : 16 * k + 16, c * CH : (c + 1) * CH] = order[
                16 * c : 16 * c + 16
            ].astype(jnp.bfloat16)
        sums = jnp.sum(order[16 * chunks :], axis=1, keepdims=True)
        sq_own[16 * k : 16 * k + 16, :] = jnp.broadcast_to(sums, (16, 128))

    swap_sq = pltpu.make_async_remote_copy(
        src_ref=sq_own,
        dst_ref=sq_peer,
        send_sem=tp_send.at[1],
        recv_sem=tp_recv.at[1],
        device_id={"tp": peer},
        device_id_type=MESH,
    )
    swap_sq.start()

    swaps = []
    for b in range(blocks):
        for part in range(2):
            copies_in[2 * b + part].wait()
            cols = pl.ds(part * hidden + b * hb, hb)
            h_own[b, :, part * hb : (part + 1) * hb] = jnp.dot(
                tokens[...], w_in[:, cols], preferred_element_type=jnp.float32
            )
        swap_h = pltpu.make_async_remote_copy(
            src_ref=h_own.at[b],
            dst_ref=h_peer.at[b],
            send_sem=h_send.at[b],
            recv_sem=h_recv.at[b],
            device_id={"tp": peer},
            device_id_type=MESH,
        )
        swap_h.start()
        swaps.append(swap_h)

    swap_sq.wait()
    mean_own = sq_own[:, :1] * (1.0 / half)
    mean_peer = sq_peer[:, :1] * (1.0 / half)
    inverse = lax.rsqrt(0.5 * mean_own + 0.5 * mean_peer + norm_eps)
    scale_own = jnp.sqrt(mean_own + norm_eps) * inverse
    scale_peer = jnp.sqrt(mean_peer + norm_eps) * inverse
    for b in range(blocks):
        swaps[b].wait()
        both = scale_own * h_own[b] + scale_peer * h_peer[b]
        gate, up = both[:, :hb], both[:, hb:]
        act[:, b * hb : (b + 1) * hb] = (gate / (1.0 + jnp.exp(-gate)) * up).astype(jnp.bfloat16)

    for c in range(chunks):
        copies_down[c].wait()
        y = jnp.dot(
            act[...], w_down[:, c * CH : (c + 1) * CH], preferred_element_type=jnp.float32
        ).astype(jnp.bfloat16)
        for k in range(ep // 8):
            y_stack[k, 16 * c : 16 * c + 16, :] = y[16 * k : 16 * k + 16]
    for k in range(ep // 8):
        order = jnp.dot(shuffle, y_stack[k], preferred_element_type=jnp.float32)
        y_packed[8 * k : 8 * k + 8] = order.astype(jnp.bfloat16).reshape(8, 16, CH)

    def back(step):
        other = lax.rem(me + step + 1, ep)
        return pltpu.make_async_remote_copy(
            src_ref=y_packed.at[other],
            dst_ref=ret.at[me],
            send_sem=back_send.at[other],
            recv_sem=back_recv.at[me],
            device_id={"ep": other},
            device_id_type=MESH,
        )

    def return_arrive(step):
        other = lax.rem(me + step + 1, ep)
        pltpu.make_async_remote_copy(
            src_ref=y_packed.at[0],
            dst_ref=ret.at[other],
            send_sem=back_send.at[other],
            recv_sem=back_recv.at[other],
            device_id={"ep": other},
            device_id_type=MESH,
        ).wait_recv()

    each(ep - 1, lambda step: back(step).start())
    ret[me] = y_packed[me]
    each(ep - 1, lambda step: go(step).wait_send())
    each(ep - 1, return_arrive)

    def combine(s):
        if pieces == 1:
            part = ret[...].reshape(EXP * 16, CH)
        else:
            part = jnp.concatenate([ret[e * pieces + s] for e in range(EXP)], axis=0)
        return jnp.dot(
            weights_hi[...], part, preferred_element_type=jnp.float32
        ) + jnp.dot(weights_lo[...], part, preferred_element_type=jnp.float32)

    result = combine(0)
    if pieces > 1:
        result = lax.fori_loop(1, pieces, lambda s, running: running + combine(s), result)
    for c in range(chunks):
        moe[:, c * CH : (c + 1) * CH] = result[c * rows : (c + 1) * rows].astype(jnp.bfloat16)
    out_moe = local(moe, moe_hbm, out_sem.at[1])
    each(ep - 1, lambda step: back(step).wait_send())
    out_stream.wait()
    out_moe.wait()


def per_device(residual, attn_partial, norm_gain, route_ids, route_scores, w_in, w_down):
    rows, half = residual.shape
    hidden = w_in.shape[2] // 2
    ep = lax.axis_size("ep")
    slots = ep * CAP
    hb = min(512, hidden)
    blocks = hidden // hb
    chunks = half // CH
    bf16, f32 = jnp.bfloat16, jnp.float32
    dma = pltpu.SemaphoreType.DMA
    anywhere = pl.BlockSpec(memory_space=pl.ANY)
    scratch = [
        pltpu.VMEM(w_in.shape[1:], bf16),
        pltpu.VMEM(w_down.shape[1:], bf16),
        pltpu.VMEM((rows, half), bf16),
        pltpu.VMEM((rows, half), bf16),
        pltpu.VMEM((rows, half), bf16),
        pltpu.VMEM((1, half), f32),
        pltpu.VMEM(route_ids.shape, jnp.int32),
        pltpu.VMEM(route_scores.shape, f32),
        pltpu.VMEM((rows, half), bf16),
        pltpu.VMEM((rows, half), bf16),
        pltpu.VMEM((8 * rows, CH), bf16),
        pltpu.VMEM((EXP, 16, CH), bf16),
        pltpu.VMEM((ep, 16, CH), bf16),
        pltpu.VMEM((slots, half), bf16),
        pltpu.VMEM((blocks, slots, 2 * hb), f32),
        pltpu.VMEM((blocks, slots, 2 * hb), f32),
        pltpu.VMEM((slots, 128), f32),
        pltpu.VMEM((slots, 128), f32),
        pltpu.VMEM((slots, hidden), bf16),
        pltpu.VMEM((ep // 8, 128, CH), bf16),
        pltpu.VMEM((ep, 16, CH), bf16),
        pltpu.VMEM((ep, 16, CH), bf16),
        pltpu.VMEM((8 * rows, EXP * 16), bf16),
        pltpu.VMEM((8 * rows, EXP * 16), bf16),
        dma((5,)),
        dma((2 * blocks,)),
        dma((chunks,)),
        dma((2,)),
        dma((2,)),
        dma((2,)),
        dma((blocks,)),
        dma((blocks,)),
        dma((ep,)),
        dma((ep,)),
        dma((ep,)),
        dma((ep,)),
    ]
    return pl.pallas_call(
        functools.partial(kernel, ep),
        out_shape=(
            jax.ShapeDtypeStruct((rows, half), bf16),
            jax.ShapeDtypeStruct((rows, half), bf16),
        ),
        in_specs=[anywhere] * 7,
        out_specs=(anywhere, anywhere),
        scratch_shapes=scratch,
        compiler_params=pltpu.CompilerParams(
            collective_id=0, has_side_effects=True, vmem_limit_bytes=56 * 1024 * 1024
        ),
        cost_estimate=pl.CostEstimate(
            flops=2 * slots * (w_in.size + w_down.size),
            bytes_accessed=2 * (w_in.size + w_down.size),
            transcendentals=slots * hidden,
        ),
    )(residual, attn_partial, norm_gain.reshape(1, half), route_ids, route_scores, w_in, w_down)


def solution(mesh):
    in_specs = (
        P(("groups", "ep"), "tp"),
        P("tp", ("groups", "ep"), None),
        P("tp"),
        P(("groups", "ep"), None),
        P(("groups", "ep"), None),
        P("ep", "tp", None),
        P("ep", None, "tp"),
    )
    out_specs = (P(("groups", "ep"), "tp"), P(("groups", "ep"), "tp"))
    return jax.shard_map(
        per_device, mesh=mesh, in_specs=in_specs, out_specs=out_specs, check_vma=False
    )
```

```python
import functools

import jax
import jax.numpy as jnp
from jax import lax
from jax.experimental import pallas as pl
from jax.experimental.pallas import tpu as pltpu
from jax.sharding import PartitionSpec as P

EXP = 8
CAP = 2
CH = 512
IN_CUTS = 8
MESH = pl.DeviceIdType.MESH

route_scale = 2.5
norm_eps = 1e-06


def iota(shape, dim):
    return lax.broadcasted_iota(jnp.int32, shape, dim)


def each(count, body):
    if count <= 8:
        for step in range(count):
            body(step)
    else:

        def run(step, carry):
            body(step)
            return carry

        lax.fori_loop(0, count, run, 0)


def split_two(value):
    high = value.astype(jnp.bfloat16)
    return high, (value - high.astype(jnp.float32)).astype(jnp.bfloat16)


def route_tables(ids, scores, rows):
    wide = 8 * rows
    spread = (iota((rows, wide), 0) == (iota((rows, wide), 1) & (rows - 1))).astype(jnp.float32)
    ids_t = jnp.dot(
        ids.astype(jnp.float32).astype(jnp.bfloat16),
        spread.astype(jnp.bfloat16),
        preferred_element_type=jnp.float32,
    )
    scores_t = jnp.dot(
        scores,
        spread,
        precision=lax.Precision.HIGHEST,
        preferred_element_type=jnp.float32,
    )
    shares = route_scale * scores_t / jnp.sum(scores_t, axis=0, keepdims=True)
    expert = iota((EXP, wide), 0).astype(jnp.float32)
    member = jnp.zeros((EXP, wide), jnp.float32)
    weight = jnp.zeros((EXP, wide), jnp.float32)
    for k in range(ids.shape[0]):
        hit = ids_t[k : k + 1, :] == expert
        member = jnp.where(hit, 1.0, member)
        weight = weight + jnp.where(hit, shares[k : k + 1, :], 0.0)
    earlier = iota((wide, wide), 0) < (iota((wide, wide), 1) & (rows - 1))
    rank = jnp.dot(
        member.astype(jnp.bfloat16),
        earlier.astype(jnp.float32).astype(jnp.bfloat16),
        preferred_element_type=jnp.float32,
    )
    code = jnp.where(member > 0.0, rank, -1.0)
    line = iota((16, wide), 0)
    same_chunk = (line >> 1) == (iota((16, wide), 1) // rows)
    want = jnp.where(same_chunk, (line & 1).astype(jnp.float32), -2.0)
    places, weighted = [], []
    for e in range(EXP):
        on = jnp.where(code[e : e + 1, :] == want, 1.0, 0.0)
        places.append(on)
        weighted.append(on * weight[e : e + 1, :])
    return jnp.concatenate(places, axis=0), jnp.concatenate(weighted, axis=0)


def kernel(
    ep,
    res_hbm, attn_hbm, gain_hbm, ids_hbm, scores_hbm, w_in_hbm, w_down_hbm,
    stream_hbm, ret, hi_hbm, lo_hbm,
    w_in, w_down, res, attn_own, attn_peer, gain, ids, scores,
    stream, stacked, packed, recv, tokens, h_own, h_peer, sq_own, sq_peer,
    running, y_stack, y_packed, weights_hi, weights_lo,
    in_sem, w_in_sem, w_down_sem, out_sem, tp_send, tp_recv,
    h_send, h_recv, go_send, go_recv, back_send, back_recv,
):
    rows, half = res.shape
    chunks = half // CH
    pieces = ep // EXP
    hidden = w_in.shape[1] // 2
    blocks, slots, _ = h_own.shape
    hb = hidden // blocks
    me = lax.axis_index("ep")
    core = lax.axis_index("tp")
    peer = 1 - core

    def local(src, dst, sem):
        copy = pltpu.make_async_copy(src, dst, sem)
        copy.start()
        return copy

    own_cols = pl.ds(pl.multiple_of(core * half, 128), half)
    peer_cols = pl.ds(pl.multiple_of(peer * half, 128), half)
    barrier = pltpu.get_barrier_semaphore()
    pl.semaphore_signal(barrier, inc=1, device_id={"tp": peer}, device_id_type=MESH)

    def greet(step):
        other = lax.rem(me + step + 1, ep)
        pl.semaphore_signal(barrier, inc=1, device_id={"ep": other}, device_id_type=MESH)

    each(ep - 1, greet)
    copy_ids = local(ids_hbm, ids, in_sem.at[0])
    copy_scores = local(scores_hbm, scores, in_sem.at[1])
    copy_attn = local(attn_hbm.at[0, :, own_cols], attn_own, in_sem.at[2])
    copy_res = local(res_hbm, res, in_sem.at[3])
    copy_gain = local(gain_hbm, gain, in_sem.at[4])
    copies_in, copies_down = [], []

    def start_down():
        for k in range(blocks):
            part = pl.ds(k * hb, hb)
            copies_down.append(local(w_down_hbm.at[0, part], w_down.at[part], w_down_sem.at[k]))

    copy_ids.wait()
    copy_scores.wait()
    place, weighted = route_tables(ids[...], scores[...], rows)
    weights_hi[...], weights_lo[...] = split_two(weighted.T)
    out_hi = local(weights_hi, hi_hbm, out_sem.at[1])
    out_lo = local(weights_lo, lo_hbm, out_sem.at[2])
    place = place.astype(jnp.bfloat16)
    side = iota((128, 128), 0)
    swapped = ((side & 14) << 3) | ((side >> 4) << 1) | (side & 1)
    shuffle = (swapped == iota((128, 128), 1)).astype(jnp.float32).astype(jnp.bfloat16)

    pl.semaphore_wait(barrier, ep)
    swap = pltpu.make_async_remote_copy(
        src_ref=attn_hbm.at[0, :, peer_cols],
        dst_ref=attn_peer,
        send_sem=tp_send.at[0],
        recv_sem=tp_recv.at[0],
        device_id={"tp": peer},
        device_id_type=MESH,
    )
    swap.start()

    for k in range(IN_CUTS):
        part = pl.ds(k * (half // IN_CUTS), half // IN_CUTS)
        copies_in.append(local(w_in_hbm.at[0, part], w_in.at[part], w_in_sem.at[k]))
    copy_attn.wait()
    copy_res.wait()
    copy_gain.wait()
    swap.wait()

    total = res[...].astype(jnp.float32) + (
        attn_own[...].astype(jnp.float32) + attn_peer[...].astype(jnp.float32)
    )
    stream[...] = total.astype(jnp.bfloat16)
    out_stream = local(stream, stream_hbm, out_sem.at[0])
    wide = stream[...].astype(jnp.float32)
    square = jnp.sum(wide * wide, axis=1, keepdims=True)
    scaled = wide * lax.rsqrt(square * (1.0 / half) + norm_eps)
    for j in range(half // 128):
        c, at = divmod(j * 128, CH)
        stacked[c * rows : (c + 1) * rows, at : at + 128] = (
            scaled[:, j * 128 : (j + 1) * 128] * gain[j : j + 1, :]
        ).astype(jnp.bfloat16)
    square = jnp.minimum(square, 3.0e38)
    first = square.astype(jnp.bfloat16).astype(jnp.float32)
    second = (square - first).astype(jnp.bfloat16).astype(jnp.float32)
    third = square - first - second
    lane = iota((rows, CH), 1)
    terms = jnp.where(
        lane == 0, first, jnp.where(lane == 1, second, jnp.where(lane == 2, third, 0.0))
    )
    stacked[chunks * rows :, :] = terms.astype(jnp.bfloat16)
    sent = jnp.dot(place, stacked[...], preferred_element_type=jnp.float32)
    packed[...] = sent.astype(jnp.bfloat16).reshape(packed.shape)

    def go(step):
        other = lax.rem(me + step + 1, ep)
        return pltpu.make_async_remote_copy(
            src_ref=packed.at[other // pieces],
            dst_ref=recv.at[me],
            send_sem=go_send.at[other],
            recv_sem=go_recv.at[me],
            device_id={"ep": other},
            device_id_type=MESH,
        )

    def arrive(step):
        other = lax.rem(me + step + 1, ep)
        pltpu.make_async_remote_copy(
            src_ref=packed.at[0],
            dst_ref=recv.at[other],
            send_sem=go_send.at[other],
            recv_sem=go_recv.at[other],
            device_id={"ep": other},
            device_id_type=MESH,
        ).wait_recv()

    each(ep - 1, lambda step: go(step).start())
    start_down()
    recv[me] = packed[me // pieces]
    y_stack[:, chunks * 16 :, :] = jnp.zeros((ep // 8, 16, CH), jnp.bfloat16)
    each(ep - 1, arrive)

    for k in range(ep // 8):
        block = recv[8 * k : 8 * k + 8].reshape(128, CH)
        order = jnp.dot(shuffle, block, preferred_element_type=jnp.float32)
        for c in range(chunks):
            tokens[16 * k : 16 * k + 16, c * CH : (c + 1) * CH] = order[
                16 * c : 16 * c + 16
            ].astype(jnp.bfloat16)
        sums = jnp.sum(order[16 * chunks :], axis=1, keepdims=True)
        sq_own[16 * k : 16 * k + 16, :] = jnp.broadcast_to(sums, (16, 128))

    swap_sq = pltpu.make_async_remote_copy(
        src_ref=sq_own,
        dst_ref=sq_peer,
        send_sem=tp_send.at[1],
        recv_sem=tp_recv.at[1],
        device_id={"tp": peer},
        device_id_type=MESH,
    )
    swap_sq.start()

    swaps = []
    for copy in copies_in:
        copy.wait()
    for b in range(blocks):
        for part in range(2):
            cols = pl.ds(part * hidden + b * hb, hb)
            h_own[b, :, part * hb : (part + 1) * hb] = jnp.dot(
                tokens[...], w_in[:, cols], preferred_element_type=jnp.float32
            )
        swap_h = pltpu.make_async_remote_copy(
            src_ref=h_own.at[b],
            dst_ref=h_peer.at[b],
            send_sem=h_send.at[b],
            recv_sem=h_recv.at[b],
            device_id={"tp": peer},
            device_id_type=MESH,
        )
        swap_h.start()
        swaps.append(swap_h)

    swap_sq.wait()
    mean_own = sq_own[:, :1] * (1.0 / half)
    mean_peer = sq_peer[:, :1] * (1.0 / half)
    inverse = lax.rsqrt(0.5 * mean_own + 0.5 * mean_peer + norm_eps)
    scale_own = jnp.sqrt(mean_own + norm_eps) * inverse
    scale_peer = jnp.sqrt(mean_peer + norm_eps) * inverse
    for b in range(blocks):
        swaps[b].wait()
        both = scale_own * h_own[b] + scale_peer * h_peer[b]
        gate, up = both[:, :hb], both[:, hb:]
        active = (gate / (1.0 + jnp.exp(-gate)) * up).astype(jnp.bfloat16)
        copies_down[b].wait()
        for c in range(chunks):
            cols = slice(c * CH, (c + 1) * CH)
            y = jnp.dot(
                active, w_down[b * hb : (b + 1) * hb, cols], preferred_element_type=jnp.float32
            )
            if b > 0:
                y = y + running[:, cols]
            if b < blocks - 1:
                running[:, cols] = y
                continue
            y = y.astype(jnp.bfloat16)
            for k in range(ep // 8):
                y_stack[k, 16 * c : 16 * c + 16, :] = y[16 * k : 16 * k + 16]
    for k in range(ep // 8):
        order = jnp.dot(shuffle, y_stack[k], preferred_element_type=jnp.float32)
        y_packed[8 * k : 8 * k + 8] = order.astype(jnp.bfloat16).reshape(8, 16, CH)

    def back(step):
        other = lax.rem(me + step + 1, ep)
        return pltpu.make_async_remote_copy(
            src_ref=y_packed.at[other],
            dst_ref=ret.at[me],
            send_sem=back_send.at[other],
            recv_sem=back_recv.at[me],
            device_id={"ep": other},
            device_id_type=MESH,
        )

    def return_arrive(step):
        other = lax.rem(me + step + 1, ep)
        pltpu.make_async_remote_copy(
            src_ref=y_packed.at[0],
            dst_ref=ret.at[other],
            send_sem=back_send.at[other],
            recv_sem=back_recv.at[other],
            device_id={"ep": other},
            device_id_type=MESH,
        ).wait_recv()

    each(ep - 1, lambda step: back(step).start())
    own_back = local(y_packed.at[me], ret.at[me], out_sem.at[3])
    each(ep - 1, lambda step: go(step).wait_send())
    each(ep - 1, return_arrive)

    each(ep - 1, lambda step: back(step).wait_send())
    own_back.wait()
    out_stream.wait()
    out_hi.wait()
    out_lo.wait()


def combine_kernel(
    pieces,
    stream_in, ret_hbm, hi_hbm, lo_hbm, stream_out, moe_hbm, stream, ret, hi, lo, moe, sem,
):
    rows, half = moe.shape
    pairs = (
        (stream_in, stream), (ret_hbm, ret), (hi_hbm, hi), (lo_hbm, lo),
    )
    copies = []
    for place, (src, dst) in enumerate(pairs):
        copies.append(pltpu.make_async_copy(src, dst, sem.at[place]))
        copies[-1].start()
    copies[0].wait()
    out_stream = pltpu.make_async_copy(stream, stream_out, sem.at[len(pairs) + 1])
    out_stream.start()
    for copy in copies[1:]:
        copy.wait()

    def combine(s):
        if pieces == 1:
            part = ret[...].reshape(EXP * 16, CH)
        else:
            part = jnp.concatenate([ret[e * pieces + s] for e in range(EXP)], axis=0)
        return jnp.dot(
            hi[...], part, preferred_element_type=jnp.float32
        ) + jnp.dot(lo[...], part, preferred_element_type=jnp.float32)

    result = combine(0)
    if pieces > 1:
        result = lax.fori_loop(1, pieces, lambda s, running: running + combine(s), result)
    for c in range(half // CH):
        moe[:, c * CH : (c + 1) * CH] = result[c * rows : (c + 1) * rows].astype(jnp.bfloat16)
    out = pltpu.make_async_copy(moe, moe_hbm, sem.at[len(pairs)])
    out.start()
    out_stream.wait()
    out.wait()


def per_device(residual, attn_partial, norm_gain, route_ids, route_scores, w_in, w_down):
    rows, half = residual.shape
    hidden = w_in.shape[2] // 2
    ep = lax.axis_size("ep")
    slots = ep * CAP
    hb = min(512, hidden)
    blocks = hidden // hb
    chunks = half // CH
    bf16, f32 = jnp.bfloat16, jnp.float32
    dma = pltpu.SemaphoreType.DMA
    anywhere = pl.BlockSpec(memory_space=pl.ANY)
    scratch = [
        pltpu.VMEM(w_in.shape[1:], bf16),
        pltpu.VMEM(w_down.shape[1:], bf16),
        pltpu.VMEM((rows, half), bf16),
        pltpu.VMEM((rows, half), bf16),
        pltpu.VMEM((rows, half), bf16),
        pltpu.VMEM((half // 128, 128), f32),
        pltpu.VMEM(route_ids.shape[::-1], jnp.int32),
        pltpu.VMEM(route_scores.shape[::-1], f32),
        pltpu.VMEM((rows, half), bf16),
        pltpu.VMEM((8 * rows, CH), bf16),
        pltpu.VMEM((EXP, 16, CH), bf16),
        pltpu.VMEM((ep, 16, CH), bf16),
        pltpu.VMEM((slots, half), bf16),
        pltpu.VMEM((blocks, slots, 2 * hb), f32),
        pltpu.VMEM((blocks, slots, 2 * hb), f32),
        pltpu.VMEM((slots, 128), f32),
        pltpu.VMEM((slots, 128), f32),
        pltpu.VMEM((slots, half), f32),
        pltpu.VMEM((ep // 8, 128, CH), bf16),
        pltpu.VMEM((ep, 16, CH), bf16),
        pltpu.VMEM((8 * rows, EXP * 16), bf16),
        pltpu.VMEM((8 * rows, EXP * 16), bf16),
        dma((5,)),
        dma((IN_CUTS,)),
        dma((blocks,)),
        dma((4,)),
        dma((2,)),
        dma((2,)),
        dma((blocks,)),
        dma((blocks,)),
        dma((ep,)),
        dma((ep,)),
        dma((ep,)),
        dma((ep,)),
    ]
    weights_shape = (8 * rows, EXP * 16)
    stream, ret, high, low = pl.pallas_call(
        functools.partial(kernel, ep),
        out_shape=(
            jax.ShapeDtypeStruct((rows, half), bf16),
            jax.ShapeDtypeStruct((ep, 16, CH), bf16),
            jax.ShapeDtypeStruct(weights_shape, bf16),
            jax.ShapeDtypeStruct(weights_shape, bf16),
        ),
        in_specs=[anywhere] * 7,
        out_specs=(anywhere,) * 4,
        scratch_shapes=scratch,
        compiler_params=pltpu.CompilerParams(
            collective_id=0, has_side_effects=True, vmem_limit_bytes=56 * 1024 * 1024
        ),
        cost_estimate=pl.CostEstimate(
            flops=2 * slots * (w_in.size + w_down.size),
            bytes_accessed=2 * (w_in.size + w_down.size),
            transcendentals=slots * hidden,
        ),
    )(
        residual,
        attn_partial,
        norm_gain.reshape(half // 128, 128),
        route_ids.T,
        route_scores.T,
        w_in,
        w_down,
    )
    return pl.pallas_call(
        functools.partial(combine_kernel, ep // EXP),
        out_shape=(
            jax.ShapeDtypeStruct((rows, half), bf16),
            jax.ShapeDtypeStruct((rows, half), bf16),
        ),
        in_specs=[anywhere] * 4,
        out_specs=(anywhere, anywhere),
        scratch_shapes=[
            pltpu.VMEM((rows, half), bf16),
            pltpu.VMEM((ep, 16, CH), bf16),
            pltpu.VMEM(weights_shape, bf16),
            pltpu.VMEM(weights_shape, bf16),
            pltpu.VMEM((rows, half), bf16),
            dma((6,)),
        ],
        cost_estimate=pl.CostEstimate(
            flops=4 * 8 * rows * ep * 16 * CH, bytes_accessed=8 * rows * half, transcendentals=0
        ),
    )(stream, ret, high, low)


def solution(mesh):
    in_specs = (
        P(("groups", "ep"), "tp"),
        P("tp", ("groups", "ep"), None),
        P("tp"),
        P(("groups", "ep"), None),
        P(("groups", "ep"), None),
        P("ep", "tp", None),
        P("ep", None, "tp"),
    )
    out_specs = (P(("groups", "ep"), "tp"), P(("groups", "ep"), "tp"))
    return jax.shard_map(
        per_device, mesh=mesh, in_specs=in_specs, out_specs=out_specs, check_vma=False
    )
```

```python
import functools

import jax
import jax.numpy as jnp
from jax import lax
from jax.experimental import pallas as pl
from jax.experimental.pallas import tpu as pltpu
from jax.sharding import PartitionSpec as P

EXP = 8
CAP = 2
CH = 512
IN_CUTS = 8
EARLY = 4
MESH = pl.DeviceIdType.MESH

route_scale = 2.5
norm_eps = 1e-06


def iota(shape, dim):
    return lax.broadcasted_iota(jnp.int32, shape, dim)


def each(count, body):
    if count <= 8:
        for step in range(count):
            body(step)
    else:

        def run(step, carry):
            body(step)
            return carry

        lax.fori_loop(0, count, run, 0)


def split_two(value):
    high = value.astype(jnp.bfloat16)
    return high, (value - high.astype(jnp.float32)).astype(jnp.bfloat16)


def route_tables(ids, scores, rows):
    wide = 8 * rows
    spread = (iota((rows, wide), 0) == (iota((rows, wide), 1) & (rows - 1))).astype(jnp.float32)
    ids_t = jnp.dot(
        ids.astype(jnp.float32).astype(jnp.bfloat16),
        spread.astype(jnp.bfloat16),
        preferred_element_type=jnp.float32,
    )
    scores_t = jnp.dot(
        scores,
        spread,
        precision=lax.Precision.HIGHEST,
        preferred_element_type=jnp.float32,
    )
    shares = route_scale * scores_t / jnp.sum(scores_t, axis=0, keepdims=True)
    expert = iota((EXP, wide), 0).astype(jnp.float32)
    member = jnp.zeros((EXP, wide), jnp.float32)
    weight = jnp.zeros((EXP, wide), jnp.float32)
    for k in range(ids.shape[0]):
        hit = ids_t[k : k + 1, :] == expert
        member = jnp.where(hit, 1.0, member)
        weight = weight + jnp.where(hit, shares[k : k + 1, :], 0.0)
    earlier = iota((wide, wide), 0) < (iota((wide, wide), 1) & (rows - 1))
    rank = jnp.dot(
        member.astype(jnp.bfloat16),
        earlier.astype(jnp.float32).astype(jnp.bfloat16),
        preferred_element_type=jnp.float32,
    )
    code = jnp.where(member > 0.0, rank, -1.0)
    line = iota((16, wide), 0)
    same_chunk = (line >> 1) == (iota((16, wide), 1) // rows)
    want = jnp.where(same_chunk, (line & 1).astype(jnp.float32), -2.0)
    places, weighted = [], []
    for e in range(EXP):
        on = jnp.where(code[e : e + 1, :] == want, 1.0, 0.0)
        places.append(on)
        weighted.append(on * weight[e : e + 1, :])
    return jnp.concatenate(places, axis=0), jnp.concatenate(weighted, axis=0)


def kernel(
    ep,
    res_hbm, attn_hbm, gain_hbm, ids_hbm, scores_hbm, w_in_hbm, w_down_hbm,
    stream_hbm, ret, hi_hbm, lo_hbm,
    w_in, w_down, res, attn_own, attn_peer, gain, ids, scores,
    stream, stacked, packed, recv, tokens, h_own, h_peer, sq_own, sq_peer,
    running, y_stack, y_packed, weights_hi, weights_lo,
    in_sem, w_in_sem, w_down_sem, out_sem, tp_send, tp_recv,
    h_send, h_recv, go_send, go_recv, back_send, back_recv,
):
    rows, half = res.shape
    chunks = half // CH
    pieces = ep // EXP
    hidden = w_in.shape[1] // 2
    blocks, slots, _ = h_own.shape
    hb = hidden // blocks
    me = lax.axis_index("ep")
    core = lax.axis_index("tp")
    peer = 1 - core

    def local(src, dst, sem):
        copy = pltpu.make_async_copy(src, dst, sem)
        copy.start()
        return copy

    own_cols = pl.ds(pl.multiple_of(core * half, 128), half)
    peer_cols = pl.ds(pl.multiple_of(peer * half, 128), half)
    barrier = pltpu.get_barrier_semaphore()
    pl.semaphore_signal(barrier, inc=1, device_id={"tp": peer}, device_id_type=MESH)

    def greet(step):
        other = lax.rem(me + step + 1, ep)
        pl.semaphore_signal(barrier, inc=1, device_id={"ep": other}, device_id_type=MESH)

    each(ep - 1, greet)
    copy_ids = local(ids_hbm, ids, in_sem.at[0])
    copy_scores = local(scores_hbm, scores, in_sem.at[1])
    copy_attn = local(attn_hbm.at[0, :, own_cols], attn_own, in_sem.at[2])
    copy_res = local(res_hbm, res, in_sem.at[3])
    copy_gain = local(gain_hbm, gain, in_sem.at[4])
    copies_in, copies_down = [], []

    def start_in(first, last):
        for k in range(first, last):
            part = pl.ds(k * (half // IN_CUTS), half // IN_CUTS)
            copies_in.append(local(w_in_hbm.at[0, part], w_in.at[part], w_in_sem.at[k]))

    def start_down():
        for k in range(blocks):
            part = pl.ds(k * hb, hb)
            copies_down.append(local(w_down_hbm.at[0, part], w_down.at[part], w_down_sem.at[k]))

    start_in(0, EARLY)
    copy_ids.wait()
    copy_scores.wait()
    place, weighted = route_tables(ids[...], scores[...], rows)
    weights_hi[...], weights_lo[...] = split_two(weighted.T)
    out_hi = local(weights_hi, hi_hbm, out_sem.at[1])
    out_lo = local(weights_lo, lo_hbm, out_sem.at[2])
    place = place.astype(jnp.bfloat16)
    side = iota((128, 128), 0)
    swapped = ((side & 14) << 3) | ((side >> 4) << 1) | (side & 1)
    shuffle = (swapped == iota((128, 128), 1)).astype(jnp.float32).astype(jnp.bfloat16)

    pl.semaphore_wait(barrier, ep)
    swap = pltpu.make_async_remote_copy(
        src_ref=attn_hbm.at[0, :, peer_cols],
        dst_ref=attn_peer,
        send_sem=tp_send.at[0],
        recv_sem=tp_recv.at[0],
        device_id={"tp": peer},
        device_id_type=MESH,
    )
    swap.start()

    start_in(EARLY, IN_CUTS)
    copy_attn.wait()
    copy_res.wait()
    copy_gain.wait()
    swap.wait()

    total = res[...].astype(jnp.float32) + (
        attn_own[...].astype(jnp.float32) + attn_peer[...].astype(jnp.float32)
    )
    stream[...] = total.astype(jnp.bfloat16)
    out_stream = local(stream, stream_hbm, out_sem.at[0])
    wide = stream[...].astype(jnp.float32)
    square = jnp.sum(wide * wide, axis=1, keepdims=True)
    scaled = wide * lax.rsqrt(square * (1.0 / half) + norm_eps)
    for j in range(half // 128):
        c, at = divmod(j * 128, CH)
        stacked[c * rows : (c + 1) * rows, at : at + 128] = (
            scaled[:, j * 128 : (j + 1) * 128] * gain[j : j + 1, :]
        ).astype(jnp.bfloat16)
    square = jnp.minimum(square, 3.0e38)
    first = square.astype(jnp.bfloat16).astype(jnp.float32)
    second = (square - first).astype(jnp.bfloat16).astype(jnp.float32)
    third = square - first - second
    lane = iota((rows, CH), 1)
    terms = jnp.where(
        lane == 0, first, jnp.where(lane == 1, second, jnp.where(lane == 2, third, 0.0))
    )
    stacked[chunks * rows :, :] = terms.astype(jnp.bfloat16)
    sent = jnp.dot(place, stacked[...], preferred_element_type=jnp.float32)
    packed[...] = sent.astype(jnp.bfloat16).reshape(packed.shape)

    def go(step):
        other = lax.rem(me + step + 1, ep)
        return pltpu.make_async_remote_copy(
            src_ref=packed.at[other // pieces],
            dst_ref=recv.at[me],
            send_sem=go_send.at[other],
            recv_sem=go_recv.at[me],
            device_id={"ep": other},
            device_id_type=MESH,
        )

    def arrive(step):
        other = lax.rem(me + step + 1, ep)
        pltpu.make_async_remote_copy(
            src_ref=packed.at[0],
            dst_ref=recv.at[other],
            send_sem=go_send.at[other],
            recv_sem=go_recv.at[other],
            device_id={"ep": other},
            device_id_type=MESH,
        ).wait_recv()

    each(ep - 1, lambda step: go(step).start())
    start_down()
    recv[me] = packed[me // pieces]
    y_stack[:, chunks * 16 :, :] = jnp.zeros((ep // 8, 16, CH), jnp.bfloat16)
    each(ep - 1, arrive)

    for k in range(ep // 8):
        block = recv[8 * k : 8 * k + 8].reshape(128, CH)
        order = jnp.dot(shuffle, block, preferred_element_type=jnp.float32)
        for c in range(chunks):
            tokens[16 * k : 16 * k + 16, c * CH : (c + 1) * CH] = order[
                16 * c : 16 * c + 16
            ].astype(jnp.bfloat16)
        sums = jnp.sum(order[16 * chunks :], axis=1, keepdims=True)
        sq_own[16 * k : 16 * k + 16, :] = jnp.broadcast_to(sums, (16, 128))

    swap_sq = pltpu.make_async_remote_copy(
        src_ref=sq_own,
        dst_ref=sq_peer,
        send_sem=tp_send.at[1],
        recv_sem=tp_recv.at[1],
        device_id={"tp": peer},
        device_id_type=MESH,
    )
    swap_sq.start()

    swaps = []
    for copy in copies_in:
        copy.wait()
    for b in range(blocks):
        for part in range(2):
            cols = pl.ds(part * hidden + b * hb, hb)
            h_own[b, :, part * hb : (part + 1) * hb] = jnp.dot(
                tokens[...], w_in[:, cols], preferred_element_type=jnp.float32
            )
        swap_h = pltpu.make_async_remote_copy(
            src_ref=h_own.at[b],
            dst_ref=h_peer.at[b],
            send_sem=h_send.at[b],
            recv_sem=h_recv.at[b],
            device_id={"tp": peer},
            device_id_type=MESH,
        )
        swap_h.start()
        swaps.append(swap_h)

    swap_sq.wait()
    mean_own = sq_own[:, :1] * (1.0 / half)
    mean_peer = sq_peer[:, :1] * (1.0 / half)
    inverse = lax.rsqrt(0.5 * mean_own + 0.5 * mean_peer + norm_eps)
    scale_own = jnp.sqrt(mean_own + norm_eps) * inverse
    scale_peer = jnp.sqrt(mean_peer + norm_eps) * inverse
    for b in range(blocks):
        swaps[b].wait()
        both = scale_own * h_own[b] + scale_peer * h_peer[b]
        gate, up = both[:, :hb], both[:, hb:]
        active = (gate / (1.0 + jnp.exp(-gate)) * up).astype(jnp.bfloat16)
        copies_down[b].wait()
        for c in range(chunks):
            cols = slice(c * CH, (c + 1) * CH)
            y = jnp.dot(
                active, w_down[b * hb : (b + 1) * hb, cols], preferred_element_type=jnp.float32
            )
            if b > 0:
                y = y + running[:, cols]
            if b < blocks - 1:
                running[:, cols] = y
                continue
            y = y.astype(jnp.bfloat16)
            for k in range(ep // 8):
                y_stack[k, 16 * c : 16 * c + 16, :] = y[16 * k : 16 * k + 16]
    for k in range(ep // 8):
        order = jnp.dot(shuffle, y_stack[k], preferred_element_type=jnp.float32)
        y_packed[8 * k : 8 * k + 8] = order.astype(jnp.bfloat16).reshape(8, 16, CH)

    def back(step):
        other = lax.rem(me + step + 1, ep)
        return pltpu.make_async_remote_copy(
            src_ref=y_packed.at[other],
            dst_ref=ret.at[me],
            send_sem=back_send.at[other],
            recv_sem=back_recv.at[me],
            device_id={"ep": other},
            device_id_type=MESH,
        )

    def return_arrive(step):
        other = lax.rem(me + step + 1, ep)
        pltpu.make_async_remote_copy(
            src_ref=y_packed.at[0],
            dst_ref=ret.at[other],
            send_sem=back_send.at[other],
            recv_sem=back_recv.at[other],
            device_id={"ep": other},
            device_id_type=MESH,
        ).wait_recv()

    each(ep - 1, lambda step: back(step).start())
    own_back = local(y_packed.at[me], ret.at[me], out_sem.at[3])
    each(ep - 1, lambda step: go(step).wait_send())
    each(ep - 1, return_arrive)

    each(ep - 1, lambda step: back(step).wait_send())
    own_back.wait()
    out_stream.wait()
    out_hi.wait()
    out_lo.wait()


def combine_kernel(
    pieces,
    stream, ret, hi, lo, stream_out, moe_hbm, moe, sem,
):
    rows, half = moe.shape
    out_stream = pltpu.make_async_copy(stream, stream_out, sem.at[0])
    out_stream.start()

    def combine(s):
        if pieces == 1:
            part = ret[...].reshape(EXP * 16, CH)
        else:
            part = jnp.concatenate([ret[e * pieces + s] for e in range(EXP)], axis=0)
        return jnp.dot(
            hi[...], part, preferred_element_type=jnp.float32
        ) + jnp.dot(lo[...], part, preferred_element_type=jnp.float32)

    result = combine(0)
    if pieces > 1:
        result = lax.fori_loop(1, pieces, lambda s, running: running + combine(s), result)
    for c in range(half // CH):
        moe[:, c * CH : (c + 1) * CH] = result[c * rows : (c + 1) * rows].astype(jnp.bfloat16)
    out = pltpu.make_async_copy(moe, moe_hbm, sem.at[1])
    out.start()
    out_stream.wait()
    out.wait()


def per_device(residual, attn_partial, norm_gain, route_ids, route_scores, w_in, w_down):
    rows, half = residual.shape
    hidden = w_in.shape[2] // 2
    ep = lax.axis_size("ep")
    slots = ep * CAP
    hb = min(512, hidden)
    blocks = hidden // hb
    chunks = half // CH
    bf16, f32 = jnp.bfloat16, jnp.float32
    dma = pltpu.SemaphoreType.DMA
    anywhere = pl.BlockSpec(memory_space=pl.ANY)
    scratch = [
        pltpu.VMEM(w_in.shape[1:], bf16),
        pltpu.VMEM(w_down.shape[1:], bf16),
        pltpu.VMEM((rows, half), bf16),
        pltpu.VMEM((rows, half), bf16),
        pltpu.VMEM((rows, half), bf16),
        pltpu.VMEM((half // 128, 128), f32),
        pltpu.VMEM(route_ids.shape[::-1], jnp.int32),
        pltpu.VMEM(route_scores.shape[::-1], f32),
        pltpu.VMEM((rows, half), bf16),
        pltpu.VMEM((8 * rows, CH), bf16),
        pltpu.VMEM((EXP, 16, CH), bf16),
        pltpu.VMEM((ep, 16, CH), bf16),
        pltpu.VMEM((slots, half), bf16),
        pltpu.VMEM((blocks, slots, 2 * hb), f32),
        pltpu.VMEM((blocks, slots, 2 * hb), f32),
        pltpu.VMEM((slots, 128), f32),
        pltpu.VMEM((slots, 128), f32),
        pltpu.VMEM((slots, half), f32),
        pltpu.VMEM((ep // 8, 128, CH), bf16),
        pltpu.VMEM((ep, 16, CH), bf16),
        pltpu.VMEM((8 * rows, EXP * 16), bf16),
        pltpu.VMEM((8 * rows, EXP * 16), bf16),
        dma((5,)),
        dma((IN_CUTS,)),
        dma((blocks,)),
        dma((4,)),
        dma((2,)),
        dma((2,)),
        dma((blocks,)),
        dma((blocks,)),
        dma((ep,)),
        dma((ep,)),
        dma((ep,)),
        dma((ep,)),
    ]
    weights_shape = (8 * rows, EXP * 16)
    stream, ret, high, low = pl.pallas_call(
        functools.partial(kernel, ep),
        out_shape=(
            jax.ShapeDtypeStruct((rows, half), bf16),
            jax.ShapeDtypeStruct((ep, 16, CH), bf16),
            jax.ShapeDtypeStruct(weights_shape, bf16),
            jax.ShapeDtypeStruct(weights_shape, bf16),
        ),
        in_specs=[pl.BlockSpec(memory_space=pltpu.HBM)] * 7,
        out_specs=(anywhere,) * 4,
        scratch_shapes=scratch,
        compiler_params=pltpu.CompilerParams(
            collective_id=0, has_side_effects=True, vmem_limit_bytes=48 * 1024 * 1024
        ),
        cost_estimate=pl.CostEstimate(
            flops=2 * slots * (w_in.size + w_down.size),
            bytes_accessed=2 * (w_in.size + w_down.size),
            transcendentals=slots * hidden,
        ),
    )(
        *(
            pltpu.with_memory_space_constraint(operand, pltpu.HBM)
            for operand in (
                residual,
                attn_partial,
                norm_gain.reshape(half // 128, 128),
                route_ids.T,
                route_scores.T,
                w_in,
                w_down,
            )
        )
    )
    return pl.pallas_call(
        functools.partial(combine_kernel, ep // EXP),
        out_shape=(
            jax.ShapeDtypeStruct((rows, half), bf16),
            jax.ShapeDtypeStruct((rows, half), bf16),
        ),
        in_specs=[pl.BlockSpec(memory_space=pltpu.VMEM)] * 4,
        out_specs=(pl.BlockSpec(memory_space=pltpu.HBM),) * 2,
        scratch_shapes=[pltpu.VMEM((rows, half), bf16), dma((2,))],
        compiler_params=pltpu.CompilerParams(vmem_limit_bytes=4 * 1024 * 1024),
        cost_estimate=pl.CostEstimate(
            flops=4 * 8 * rows * ep * 16 * CH, bytes_accessed=8 * rows * half, transcendentals=0
        ),
    )(stream, ret, high, low)


def solution(mesh):
    in_specs = (
        P(("groups", "ep"), "tp"),
        P("tp", ("groups", "ep"), None),
        P("tp"),
        P(("groups", "ep"), None),
        P(("groups", "ep"), None),
        P("ep", "tp", None),
        P("ep", None, "tp"),
    )
    out_specs = (P(("groups", "ep"), "tp"), P(("groups", "ep"), "tp"))
    return jax.shard_map(
        per_device, mesh=mesh, in_specs=in_specs, out_specs=out_specs, check_vma=False
    )
```
